32 devices in a mesh: wave: 8 (over z, x), lev: 4 (over y, core).
Axes of the slice: x: 2, y: 2, z: 4, core: 2. Of those that a mesh axis runs over, the one named last changes fastest.
Arguments:
- grid: float32 [4, 640, 1344], P(None, 'lev', 'wave'), may hold values from -6 to 6
- row_points: int32 [640], replicated, may hold values from 20 to 1344, as said below
- lat_of_slot: int32 [640], replicated, may hold values from 0 to 639, each once
- pair_low: int32 [320], replicated, may hold values from 0 to 319, each once
- legendre: float32 [320, 205120], P(None, 'wave'), may hold values from -6 to 6
- lat_weight: float32 [320], replicated, may hold values from 0.02 to 0.2
- vert_modes: float32 [4, 4], replicated, may hold values from -3 to 3
- vert_back: float32 [4, 4], replicated, may hold values from -3 to 3
- vert_rates: float32 [4], replicated, may hold values from 0.5 to 20
Outputs:
- spectral: float32 [4, 2, 205824], P('lev', None, 'wave')
- grid_out: float32 [4, 640, 1344], P(None, 'lev', 'wave')
The draws below stay inside these ranges and needn't reach their ends.
Inputs may be any that keep to these rules, and one draw needn't show every extreme that they name: row_points[r] is the number of points of the row of latitude r; it is even and equal to row_points[639 - r]. A permutation: row slot s holds latitude lat_of_slot[s]. A permutation: pair position g holds wavenumbers pair_low[g] and 639 - pair_low[g].
All inputs are finite; a program needn't handle non-finite values.
Results may differ from the reference program's by a relative error of at most 0.000084.
Values sent between devices are 32-bit elements; how exact they have to be, the bound alone decides.
A program may use at most 256 MiB of HBM per device.

```python
import math
import jax
import jax.numpy as jnp
from jax import lax

NLAT = 640
LEVELS = 4
HALF = 320
PAIRS_DEV = 40
MAXPTS = 1344
MODES_PAD = 25728
N_WAVE = 8


def draw_row_points(key, part):
    half_rows = NLAT // 2
    index_rows = jnp.arange(half_rows, dtype=jnp.int32)
    jitter = jax.random.randint(key, (half_rows,), 0, 8, dtype=jnp.int32)
    jitter = jnp.where(index_rows == 0, 0, jitter)
    north_len = 20 + 4 * index_rows + 4 * jitter
    north_len = jnp.minimum(north_len, MAXPTS)
    north_len = jnp.where(index_rows == half_rows - 1, MAXPTS, north_len)
    return jnp.concatenate([north_len, north_len[::-1]]).astype(jnp.int32)


def levels(key, dims, cuts, least, top_value):
    gain, own = 1.0, jax.random.fold_in(key, 6)
    for axis_at, shards_of in cuts:
        steps = jnp.exp(jax.random.uniform(jax.random.fold_in(own, axis_at), (shards_of,), jnp.float32, least / len(cuts), top_value / len(cuts)))
        gain = gain * jnp.repeat(steps, dims[axis_at] // shards_of).reshape([-1 if axis == axis_at else 1 for axis in range(len(dims))])
    return gain


def scatter_about(stream_key, dims, scale, reach, split=(), held_as=jnp.bfloat16):
    loudness = levels(stream_key, dims, split, -0.22, 0.18) if split else 1.0
    drawn = jax.random.normal(stream_key, dims, jnp.float32) * scale * loudness
    return jnp.minimum(jnp.maximum(drawn, -reach), reach).astype(held_as)


def setup_inputs(seed: int = 0) -> dict:
    streams_of = jax.random.split(jax.random.key(seed), 10)
    grid = scatter_about(streams_of[0], (LEVELS, NLAT, MAXPTS), 1.0, 6.0, ((1, 4), (2, 8)), jnp.float32)
    row_points = draw_row_points(jax.random.fold_in(streams_of[9], 71), 0)
    lat_of_slot = jax.random.permutation(streams_of[2], NLAT).astype(jnp.int32)
    pair_low = jax.random.permutation(streams_of[3], NLAT // 2).astype(jnp.int32)
    legendre = scatter_about(streams_of[4], (HALF, N_WAVE * PAIRS_DEV * (NLAT + 1)), 1.0, 6.0, ((1, 8),), jnp.float32)
    lat_weight = jnp.clip(jnp.exp(jax.random.uniform(streams_of[5], (HALF,), jnp.float32, math.log(0.02), math.log(0.2))), 0.02, 0.2)
    vert_modes = scatter_about(streams_of[6], (LEVELS, LEVELS), LEVELS ** -0.5, 3.0, (), jnp.float32)
    vert_back = scatter_about(streams_of[7], (LEVELS, LEVELS), LEVELS ** -0.5, 3.0, (), jnp.float32)
    vert_rates = jnp.clip(jnp.exp(jax.random.uniform(streams_of[8], (LEVELS,), jnp.float32, math.log(0.5), math.log(20.0))), 0.5, 20.0)
    return {"grid": grid, "row_points": row_points, "lat_of_slot": lat_of_slot, "pair_low": pair_low, "legendre": legendre, "lat_weight": lat_weight, "vert_modes": vert_modes, "vert_back": vert_back, "vert_rates": vert_rates}


TWO_PI = 2.0 * math.pi
PRECISE = lax.Precision.HIGHEST

def row_tables(row_length, inner_len, outer_len, waves):
    length_int = row_length[:, None, None]
    length_flt = length_int.astype(jnp.float32)
    wavenum = jnp.arange(waves, dtype=jnp.int32)[None, None, :]
    inner_idx = jnp.arange(inner_len, dtype=jnp.int32)[None, :, None]
    outer_idx = jnp.arange(outer_len, dtype=jnp.int32)[None, :, None]
    inner_angle = (wavenum * inner_idx % length_int).astype(jnp.float32) * TWO_PI / length_flt
    outer_angle = (wavenum * (outer_idx * inner_len) % length_int).astype(jnp.float32) * TWO_PI / length_flt
    return (jnp.cos(inner_angle), jnp.sin(inner_angle), jnp.cos(outer_angle), jnp.sin(outer_angle))

def wave_keep(row_length, waves):
    wavenum = jnp.arange(waves, dtype=jnp.int32)[None, :]
    keeper = (2 * wavenum < row_length[:, None]).astype(jnp.float32)
    return keeper * lax.rsqrt(row_length.astype(jnp.float32))[:, None]

def forward_dft(grid_rows, row_length, waves):
    vectors, row_count, length = grid_rows.shape
    inner_len = 32
    outer_len = length // inner_len
    live_mask = (jnp.arange(length, dtype=jnp.int32)[None, :] < row_length[:, None]).astype(jnp.float32)
    blocks = (grid_rows * live_mask[None]).reshape(vectors, row_count, outer_len, inner_len)
    cos_in, sin_in, cos_out, sin_out = row_tables(row_length, inner_len, outer_len, waves)
    first_real = jnp.einsum('vsoj,sjm->vsom', blocks, cos_in, precision=PRECISE)
    first_imaginary = -jnp.einsum('vsoj,sjm->vsom', blocks, sin_in, precision=PRECISE)
    fourier_real = lax.optimization_barrier(jnp.sum(first_real * cos_out[None] + first_imaginary * sin_out[None], axis=2))
    fourier_imaginary = lax.optimization_barrier(jnp.sum(first_imaginary * cos_out[None] - first_real * sin_out[None], axis=2))
    keeper = wave_keep(row_length, waves)[None]
    return (fourier_real * keeper, fourier_imaginary * keeper)

def inverse_dft(fourier_real, fourier_imaginary, row_length, length):
    vectors, row_count, waves = fourier_real.shape
    inner_len = 32
    outer_len = length // inner_len
    cos_in, sin_in, cos_out, sin_out = row_tables(row_length, inner_len, outer_len, waves)
    doubled = jnp.where(jnp.arange(waves, dtype=jnp.int32) == 0, 1.0, 2.0).astype(jnp.float32)
    weight_row = wave_keep(row_length, waves) * doubled[None, :]
    scaled_real = (fourier_real * weight_row[None])[:, :, None, :]
    scaled_imaginary = (fourier_imaginary * weight_row[None])[:, :, None, :]
    turned_real = scaled_real * cos_out[None] - scaled_imaginary * sin_out[None]
    turned_imaginary = scaled_real * sin_out[None] + scaled_imaginary * cos_out[None]
    values = jnp.einsum('vsom,sjm->vsoj', turned_real, cos_in, precision=PRECISE)
    values = values - jnp.einsum('vsom,sjm->vsoj', turned_imaginary, sin_in, precision=PRECISE)
    live_mask = (jnp.arange(length, dtype=jnp.int32)[None, :] < row_length[:, None]).astype(jnp.float32)
    return values.reshape(vectors, row_count, length) * live_mask[None]

def mode_select(low_waves, waves):
    column = jnp.arange(waves + 1, dtype=jnp.int32)[None, :]
    low_length = (waves - low_waves)[:, None]
    upper = column >= low_length
    parity = jnp.where(upper, column - low_length, column) % 2
    half_sel = jnp.arange(2, dtype=jnp.int32)[None, :, None, None]
    parity_sel = jnp.arange(2, dtype=jnp.int32)[None, None, :, None]
    chosen = (upper.astype(jnp.int32)[:, None, None, :] == half_sel) & (parity[:, None, None, :] == parity_sel)
    return chosen.astype(jnp.float32)

def mode_degree(low_waves, waves):
    column = jnp.arange(waves + 1, dtype=jnp.int32)[None, :]
    low_length = (waves - low_waves)[:, None]
    return jnp.where(column < low_length, low_waves[:, None] + column, column - 1).astype(jnp.int32)

def pack_modes(values):
    leading = values.shape[0]
    blocks = values.reshape(leading, N_WAVE, PAIRS_DEV * (NLAT + 1))
    blocks = jnp.pad(blocks, ((0, 0), (0, 0), (0, MODES_PAD - PAIRS_DEV * (NLAT + 1))))
    return blocks.reshape(leading, N_WAVE * MODES_PAD)

def reference(grid, row_points, lat_of_slot, pair_low, legendre, lat_weight, vert_modes, vert_back, vert_rates):
    waves = NLAT
    slot_points = jnp.take(row_points, lat_of_slot).astype(jnp.int32)
    positions = jnp.arange(NLAT, dtype=jnp.int32)
    slot_of_lat = jnp.zeros((NLAT,), jnp.int32).at[lat_of_slot].set(positions)
    wave_order = jnp.stack([pair_low, waves - 1 - pair_low], axis=1).reshape(waves).astype(jnp.int32)
    inverse_order = jnp.zeros((waves,), jnp.int32).at[wave_order].set(jnp.arange(waves, dtype=jnp.int32))
    mode_sel = mode_select(pair_low, waves)
    legendre_cols = legendre.reshape(HALF, NLAT // 2, waves + 1)
    weight = lat_weight[:, None]

    def analyse(level_rows):
        fourier_real, fourier_imaginary = forward_dft(level_rows[None], slot_points, waves)
        fourier = jnp.concatenate([fourier_real, fourier_imaginary], axis=0)
        by_latitude = jnp.take(fourier, slot_of_lat, axis=1)
        north_rows = by_latitude[:, :HALF]
        south_rows = jnp.flip(by_latitude[:, HALF:], axis=1)
        symmetric = jnp.take((north_rows + south_rows) * weight, wave_order, axis=2)
        antisymmetric = jnp.take((north_rows - south_rows) * weight, wave_order, axis=2)
        combined = jnp.stack([symmetric, antisymmetric], axis=-1).reshape(2, HALF, NLAT // 2, 2, 2)
        projected = jnp.einsum('cigha,igp->cghap', combined, legendre_cols, precision=PRECISE)
        spectra = lax.optimization_barrier(jnp.sum(projected * mode_sel[None], axis=(2, 3)))
        return pack_modes(spectra)
    raw_spectra = lax.map(analyse, grid)
    degree = pack_modes(mode_degree(pair_low, waves).astype(jnp.float32)[None])[0]
    eigen_term = degree * (degree + 1.0) / float(waves * waves)
    damping = 1.0 / (1.0 + vert_rates[:, None] * eigen_term[None, :])
    projected = jnp.einsum('kj,jcm->kcm', vert_modes, raw_spectra, precision=PRECISE) * damping[:, None, :]
    spectral = jnp.einsum('lk,kcm->lcm', vert_back, projected, precision=PRECISE)
    back_scale = 1.0 / math.sqrt(waves)

    def synthesise(level_spec):
        coefficients = level_spec.reshape(2, N_WAVE, MODES_PAD)[:, :, :PAIRS_DEV * (waves + 1)]
        coefficients = coefficients.reshape(2, NLAT // 2, waves + 1)
        parts = coefficients[:, :, None, None, :] * mode_sel[None]
        by_parity = jnp.einsum('cghap,igp->cigha', parts, legendre_cols, precision=PRECISE) * back_scale
        north_rows = (by_parity[..., 0] + by_parity[..., 1]).reshape(2, HALF, waves)
        south_rows = (by_parity[..., 0] - by_parity[..., 1]).reshape(2, HALF, waves)
        whole_lat = jnp.concatenate([north_rows, jnp.flip(south_rows, axis=1)], axis=1)
        whole_lat = jnp.take(whole_lat, inverse_order, axis=2)
        by_slot = jnp.take(whole_lat, lat_of_slot, axis=1)
        return inverse_dft(by_slot[0][None], by_slot[1][None], slot_points, MAXPTS)[0]
    grid_out = lax.map(synthesise, spectral)
    return (spectral, grid_out)
```

```python
import functools
import math

import jax
import jax.numpy as jnp
import numpy as np
from jax import lax
from jax.experimental import pallas as pl
from jax.experimental.pallas import tpu as pltpu
from jax.sharding import PartitionSpec as P

HIGHEST = lax.Precision.HIGHEST
BOTH = ("wave", "lev")
INNER = 64
WIDTH = 512
NN = (((1,), (0,)), ((), ()))
NT = (((1,), (1,)), ((), ()))


def half_turn_fit():
    nodes = 0.5 * np.cos(np.pi * (np.arange(400) + 0.5) / 800)
    square = nodes**2
    sine = np.linalg.lstsq(
        np.vander(square, 5, increasing=True), np.sin(np.pi * nodes) / nodes, rcond=None
    )[0]
    cosine = np.linalg.lstsq(
        np.vander(square, 6, increasing=True), np.cos(np.pi * nodes), rcond=None
    )[0]
    return [round(float(c), 10) for c in sine], [round(float(c), 10) for c in cosine]


SINE, COSINE = half_turn_fit()


def poly(coefs, square):
    total = coefs[-1] * square + coefs[-2]
    for c in coefs[-3::-1]:
        total = total * square + c
    return total


def turn(product, length, inverse):
    rest = product - jnp.floor(product * inverse + 0.5) * length
    part = rest * inverse
    square = part * part
    sine = poly(SINE, square) * part
    cosine = poly(COSINE, square)
    double = sine + sine
    return 1.0 - double * sine, double * cosine


def halves(x):
    high = x.astype(jnp.bfloat16)
    return high, (x - high.astype(jnp.float32)).astype(jnp.bfloat16)


def both_halves(x):
    high = x.astype(jnp.bfloat16).astype(jnp.float32)
    return jnp.concatenate([high, x - high], axis=0).astype(jnp.bfloat16), high.astype(jnp.bfloat16)


def dot(a, b, dims):
    return lax.dot_general(a, b, dims, preferred_element_type=jnp.float32)


def dot_split(stacked, high, b_high, b_low, dims):
    rows = high.shape[0]
    first = dot(stacked, b_high, dims)
    return first[:rows] + first[rows:] + dot(high, b_low, dims)


def row_iota(rows):
    return lax.broadcasted_iota(jnp.int32, (rows, 1), 0)


def live_mask(length, vectors, outer):
    row = row_iota(vectors * outer) % outer
    position = row * INNER + lax.broadcasted_iota(jnp.int32, (vectors * outer, INNER), 1)
    return (position.astype(jnp.float32) < length).astype(jnp.float32)


def tables(wave, length, inverse, outer):
    inner_idx = row_iota(INNER).astype(jnp.float32)
    outer_idx = (row_iota(outer) * INNER).astype(jnp.float32)
    return turn(inner_idx * wave, length, inverse) + turn(outer_idx * wave, length, inverse)


def forward_kernel(vectors, outer, facts, x_ref, wave_ref, out_ref):
    def one(r, carry):
        length, inverse, norm = facts[0, r], facts[1, r], facts[2, r]
        wave = wave_ref[...]
        cos_in, sin_in, cos_out, sin_out = tables(wave, length, inverse, outer)
        x = x_ref[r] * live_mask(length, vectors, outer)
        stacked, high = both_halves(x)
        along = dot_split(stacked, high, *halves(cos_in), NN)
        across = dot_split(stacked, high, *halves(sin_in), NN)
        keep = jnp.where(wave + wave < length, norm, 0.0)
        rows = []
        for v in range(vectors):
            p, q = along[v * outer : (v + 1) * outer], across[v * outer : (v + 1) * outer]
            rows.append(jnp.sum(p * cos_out - q * sin_out, axis=0, keepdims=True) * keep)
            rows.append(jnp.sum(q * cos_out + p * sin_out, axis=0, keepdims=True) * -keep)
        out_ref[r] = jnp.concatenate(rows, axis=0)
        return carry

    lax.fori_loop(0, x_ref.shape[0], one, 0)


def inverse_kernel(vectors, outer, scale, facts, f_ref, wave_ref, out_ref):
    def one(r, carry):
        length, inverse, norm = facts[0, r], facts[1, r], facts[2, r]
        wave = wave_ref[...]
        cos_in, sin_in, cos_out, sin_out = tables(wave, length, inverse, outer)
        weight = jnp.where(wave + wave < length, norm * scale, 0.0)
        weight = weight * jnp.where(wave == 0.0, 1.0, 2.0)
        four = f_ref[r] * weight
        real, imaginary = [], []
        for v in range(vectors):
            a, b = four[2 * v : 2 * v + 1], four[2 * v + 1 : 2 * v + 2]
            real.append(a * cos_out - b * sin_out)
            imaginary.append(-(a * sin_out + b * cos_out))
        values = dot_split(*both_halves(jnp.concatenate(real, axis=0)), *halves(cos_in), NT)
        values += dot_split(*both_halves(jnp.concatenate(imaginary, axis=0)), *halves(sin_in), NT)
        out_ref[r] = values * live_mask(length, vectors, outer)
        return carry

    lax.fori_loop(0, f_ref.shape[0], one, 0)


def legendre_kernel(
    waves, used, span, place, low, four_ref, leg_ref, modes_ref, back_ref, rates_ref, spec_ref, out_ref
):
    step = pl.program_id(0)
    rows = four_ref.shape[1]
    fields = rows // 4
    pair_total = low.shape[0]
    first_pair = place[1]

    @pl.when(step == 0)
    def _():
        out_ref[...] = jnp.zeros_like(out_ref)

    base = (place[0] + step) * WIDTH
    pair = base // (waves + 1)
    column = base + lax.broadcasted_iota(jnp.int32, (1, WIDTH), 1)
    second = column >= (pair + 1) * (waves + 1)
    own_pair = jnp.where(second, pair + 1, pair)
    last = pair_total - 1
    low_wave = jnp.where(
        second, low[jnp.minimum(pair + 1, last)], low[jnp.minimum(pair, last)]
    )
    inside = column - own_pair * (waves + 1)
    low_length = waves - low_wave
    upper = inside >= low_length
    kind = jnp.where(upper, 2 + ((inside - low_length) & 1), inside & 1)
    degree = jnp.where(upper, inside - 1, low_wave + inside).astype(jnp.float32)
    valid = (own_pair >= first_pair) & (own_pair < first_pair + span) & (column < used)
    kind = jnp.where(valid, jnp.where(second, kind + 4, kind), 8)
    masks = [(kind == s).astype(jnp.float32) for s in range(8)]

    here = jnp.clip(pair - first_pair, 0, span - 1)
    there = jnp.clip(pair + 1 - first_pair, 0, span - 1)
    leg = jnp.where(column < used, leg_ref[...], 0.0)
    leg_high, leg_low = halves(leg)
    four = jnp.concatenate([four_ref[here], four_ref[there]], axis=0)
    product = dot_split(*both_halves(four), leg_high, leg_low, NN)
    raw = masks[0] * product[:fields]
    for s in range(1, 8):
        raw += masks[s] * product[s * fields : (s + 1) * fields]

    def mix(matrix, values):
        return lax.dot_general(
            matrix, values, NN, precision=HIGHEST, preferred_element_type=jnp.float32
        )

    eigen = degree * (degree + 1.0) * (1.0 / (waves * waves))
    projected = mix(modes_ref[...], raw) / (1.0 + rates_ref[...] * eigen)
    spectral = mix(back_ref[...], projected)
    spec_ref[...] = spectral
    parts = jnp.concatenate([masks[s] * spectral for s in range(8)], axis=0)
    sums = dot_split(*both_halves(parts), leg_high, leg_low, NT)
    out_ref[here] += sums[:rows]
    out_ref[there] += sums[rows:]


def smem():
    return pl.BlockSpec(memory_space=pltpu.SMEM)


def vmem():
    return pl.BlockSpec(memory_space=pltpu.VMEM)


def exchange(blocks, axes):
    shape = blocks.shape
    count = math.prod(shape[1:])
    dense = (shape[0], count // 128, 128) if count % 128 == 0 else (shape[0], 1, count)
    sent = lax.all_to_all(blocks.reshape(dense), axes, split_axis=0, concat_axis=0, tiled=True)
    return sent.reshape(shape)


def body(
    n_wave, n_lev, grid, row_points, lat_of_slot, pair_low, legendre, lat_weight, vert_modes, vert_back, vert_rates
):
    levels = grid.shape[0]
    ld = levels // n_lev
    waves = lat_of_slot.shape[0]
    half = waves // 2
    points = grid.shape[2] * n_wave
    lats = half // n_wave
    pair_count = legendre.shape[1] // (waves + 1)
    used = pair_count * (waves + 1)
    modes_pad = (used + 127) // 128 * 128
    span = -(-pair_count // n_lev)
    outer = -(-points // (INNER * 8)) * 8
    vectors = 2 * ld
    fields = 2 * levels
    devices = n_wave * n_lev
    wave_index = lax.axis_index("wave")
    lev_index = lax.axis_index("lev")

    low_blocks = pair_low.reshape(n_wave, pair_count)
    order = jnp.stack([low_blocks, waves - 1 - low_blocks], axis=2)
    order = jnp.pad(
        order, ((0, 0), (0, n_lev * span - pair_count), (0, 0)), constant_values=points
    )
    order = order.reshape(1, devices * span * 2).astype(jnp.float32)
    columns = order.shape[1]
    my_points = lax.dynamic_slice_in_dim(row_points, wave_index * lats, lats).astype(jnp.float32)
    facts = jnp.stack([my_points, 1.0 / my_points, lax.rsqrt(my_points)])

    lat_idx = jnp.arange(half, dtype=jnp.int32)[:, None]
    north = (lat_of_slot[None, :] == lat_idx).astype(jnp.float32)
    south = (lat_of_slot[None, :] == waves - 1 - lat_idx).astype(jnp.float32)
    unfold = jnp.stack([north + south, north - south], axis=1)
    fold = (unfold * lat_weight[:, None, None]).reshape(waves, waves)
    unfold = unfold.reshape(waves, waves)

    whole = lax.all_to_all(grid, "lev", split_axis=0, concat_axis=1, tiled=True)
    folded = jnp.einsum("xs,lsj->lxj", fold, whole, precision=HIGHEST)
    rows_in = lax.all_to_all(folded, "wave", split_axis=1, concat_axis=2, tiled=True)
    rows_in = rows_in.reshape(ld, lats, 2, points).transpose(1, 2, 0, 3)
    rows_in = jnp.pad(rows_in, ((0, 0), (0, 0), (0, 0), (0, outer * INNER - points)))
    rows_in = rows_in.reshape(lats, vectors * outer, INNER)

    params = pltpu.CompilerParams(vmem_limit_bytes=48 * 1024 * 1024)
    fourier = pl.pallas_call(
        functools.partial(forward_kernel, vectors, outer),
        out_shape=jax.ShapeDtypeStruct((lats, 2 * vectors, columns), jnp.float32),
        in_specs=[smem(), vmem(), vmem()],
        out_specs=vmem(),
        compiler_params=params,
        name="forward_rows",
    )(facts, rows_in, order)

    fourier = fourier.reshape(lats, 2, ld, 2, devices, 2 * span).transpose(4, 5, 1, 2, 3, 0)
    arrived = exchange(fourier, BOTH).reshape(n_wave, n_lev, span, 2, 2, ld, 2, lats)
    four = arrived.transpose(2, 3, 4, 1, 5, 6, 0, 7).reshape(span, 4 * fields, half)

    starts = [min(l * span * (waves + 1), used - 1) // WIDTH for l in range(n_lev)]
    stops = [-(-min((l + 1) * span * (waves + 1), used) // WIDTH) for l in range(n_lev)]
    steps = max(1, max(b - a for a, b in zip(starts, stops)))
    final_block = (used - 1) // WIDTH
    start = jnp.minimum(lev_index * span * (waves + 1), used - 1) // WIDTH
    place = jnp.stack([start, lev_index * span]).astype(jnp.int32)
    my_low = lax.dynamic_slice_in_dim(pair_low, wave_index * pair_count, pair_count)
    pair_eye = jnp.eye(2, dtype=jnp.float32)
    grow = lambda m: (m[:, None, :, None] * pair_eye[None, :, None, :]).reshape(fields, fields)
    rates = jnp.repeat(vert_rates, 2)[:, None]
    fixed = lambda *shape: pl.BlockSpec(shape, lambda t, *_: (0,) * len(shape))
    spec, back = pl.pallas_call(
        functools.partial(legendre_kernel, waves, used, span),
        out_shape=(
            jax.ShapeDtypeStruct((fields, steps * WIDTH), jnp.float32),
            jax.ShapeDtypeStruct((span, 4 * fields, half), jnp.float32),
        ),
        grid_spec=pltpu.PrefetchScalarGridSpec(
            num_scalar_prefetch=2,
            grid=(steps,),
            in_specs=[
                fixed(span, 4 * fields, half),
                pl.BlockSpec(
                    (half, WIDTH), lambda t, p, _: (0, jnp.minimum(p[0] + t, final_block))
                ),
                fixed(fields, fields),
                fixed(fields, fields),
                fixed(fields, 1),
            ],
            out_specs=[
                pl.BlockSpec((fields, WIDTH), lambda t, *_: (0, t)),
                fixed(span, 4 * fields, half),
            ],
        ),
        compiler_params=params,
        name="legendre_both",
    )(place, my_low, four, legendre, grow(vert_modes), grow(vert_back), rates)

    pieces = lax.all_to_all(
        spec.reshape(n_lev, fields // n_lev, steps * WIDTH), "lev", split_axis=0, concat_axis=0, tiled=True
    )
    full = (final_block + 1 + steps) * WIDTH
    spectral = sum(
        jnp.pad(pieces[l], ((0, 0), (starts[l] * WIDTH, full - (starts[l] + steps) * WIDTH)))
        for l in range(n_lev)
    )
    spectral = spectral[:, :modes_pad].reshape(ld, 2, modes_pad)

    back = back.reshape(span, 2, 2, n_lev, ld, 2, n_wave, lats).transpose(6, 3, 0, 1, 2, 4, 5, 7)
    returned = exchange(back.reshape(devices, 2 * span, 2, ld, 2, lats), BOTH)
    returned = returned.transpose(5, 2, 3, 4, 0, 1).reshape(lats, 2 * vectors, columns)
    values = pl.pallas_call(
        functools.partial(inverse_kernel, vectors, outer, 1.0 / math.sqrt(waves)),
        out_shape=jax.ShapeDtypeStruct((lats, vectors * outer, INNER), jnp.float32),
        in_specs=[smem(), vmem(), vmem()],
        out_specs=vmem(),
        compiler_params=params,
        name="inverse_rows",
    )(facts, returned, order)
    values = values.reshape(lats, 2, ld, outer * INNER)[..., :points]
    values = values.transpose(2, 0, 1, 3).reshape(ld, 2 * lats, points)
    values = lax.all_to_all(values, "wave", split_axis=2, concat_axis=1, tiled=True)
    slots = jnp.einsum("xs,lxj->lsj", unfold, values, precision=HIGHEST)
    grid_out = lax.all_to_all(slots, "lev", split_axis=1, concat_axis=0, tiled=True)
    return spectral, grid_out


def solution(mesh):
    placed = (P(None, "lev", "wave"), P(), P(), P(), P(None, "wave"), P(), P(), P(), P())
    return jax.shard_map(
        functools.partial(body, mesh.shape["wave"], mesh.shape["lev"]),
        mesh=mesh,
        in_specs=placed,
        out_specs=(P("lev", None, "wave"), P(None, "lev", "wave")),
        check_vma=False,
    )
```

```python
import functools
import math

import jax
import jax.numpy as jnp
import numpy as np
from jax import lax
from jax.experimental import pallas as pl
from jax.experimental.pallas import tpu as pltpu
from jax.sharding import PartitionSpec as P

HIGHEST = lax.Precision.HIGHEST
BOTH = ("wave", "lev")
INNER = 64
WIDTH = 640
NN = (((1,), (0,)), ((), ()))
NT = (((1,), (1,)), ((), ()))


def half_turn_fit():
    nodes = 0.5 * np.cos(np.pi * (np.arange(400) + 0.5) / 800)
    square = nodes**2
    sine = np.linalg.lstsq(
        np.vander(square, 5, increasing=True), np.sin(np.pi * nodes) / nodes, rcond=None
    )[0]
    cosine = np.linalg.lstsq(
        np.vander(square, 6, increasing=True), np.cos(np.pi * nodes), rcond=None
    )[0]
    return [round(float(c), 10) for c in sine], [round(float(c), 10) for c in cosine]


SINE, COSINE = half_turn_fit()


def poly(coefs, square):
    total = coefs[-1] * square + coefs[-2]
    for c in coefs[-3::-1]:
        total = total * square + c
    return total


def turn(product, length, inverse):
    rest = product - jnp.floor(product * inverse + 0.5) * length
    part = rest * inverse
    square = part * part
    sine = poly(SINE, square) * part
    cosine = poly(COSINE, square)
    double = sine + sine
    return 1.0 - double * sine, double * cosine


def halves(x):
    high = x.astype(jnp.bfloat16)
    return high, (x - high.astype(jnp.float32)).astype(jnp.bfloat16)


def both_halves(x):
    high = x.astype(jnp.bfloat16).astype(jnp.float32)
    return jnp.concatenate([high, x - high], axis=0).astype(jnp.bfloat16), high.astype(jnp.bfloat16)


def dot(a, b, dims):
    return lax.dot_general(a, b, dims, preferred_element_type=jnp.float32)


def dot_split(stacked, high, b_high, b_low, dims):
    rows = high.shape[0]
    first = dot(stacked, b_high, dims)
    return first[:rows] + first[rows:] + dot(high, b_low, dims)


def row_iota(rows):
    return lax.broadcasted_iota(jnp.int32, (rows, 1), 0)


def live_mask(length, vectors, outer):
    row = row_iota(vectors * outer) % outer
    position = row * INNER + lax.broadcasted_iota(jnp.int32, (vectors * outer, INNER), 1)
    return (position.astype(jnp.float32) < length).astype(jnp.float32)


def angle_sums(cos_base, sin_base, cos_step, sin_step):
    cos_rows, sin_rows = [], []
    for k in range(cos_step.shape[0]):
        c, s = cos_step[k : k + 1], sin_step[k : k + 1]
        cos_rows.append(cos_base * c - sin_base * s)
        sin_rows.append(sin_base * c + cos_base * s)
    return jnp.concatenate(cos_rows, axis=0), jnp.concatenate(sin_rows, axis=0)


def tables(wave, length, inverse, outer):
    row = row_iota(32)
    scale = jnp.where(row < 16, jnp.where(row < 8, 1, 8), jnp.where(row < 24, 64, 512))
    multiple = ((row & 7) * scale).astype(jnp.float32)
    c, s = turn(multiple * wave, length, inverse)
    top = 24 + outer // 8
    return angle_sums(c[:8], s[:8], c[8:16], s[8:16]) + angle_sums(
        c[16:24], s[16:24], c[24:top], s[24:top]
    )


def each_row(rows, one):
    together = 2 if rows % 2 == 0 else 1

    def some(step, carry):
        for k in range(together):
            one(step * together + k)
        return carry

    lax.fori_loop(0, rows // together, some, 0)


def forward_kernel(vectors, outer, facts, x_ref, wave_ref, out_ref):
    def one(r):
        length, inverse, norm = facts[0, r], facts[1, r], facts[2, r]
        wave = wave_ref[...]
        cos_in, sin_in, cos_out, sin_out = tables(wave, length, inverse, outer)
        x = x_ref[r] * live_mask(length, vectors, outer)
        stacked, high = both_halves(x)
        along = dot_split(stacked, high, *halves(cos_in), NN)
        across = dot_split(stacked, high, *halves(sin_in), NN)
        keep = jnp.where(wave + wave < length, norm, 0.0)
        rows = []
        for v in range(vectors):
            p, q = along[v * outer : (v + 1) * outer], across[v * outer : (v + 1) * outer]
            rows.append(jnp.sum(p * cos_out - q * sin_out, axis=0, keepdims=True) * keep)
            rows.append(jnp.sum(q * cos_out + p * sin_out, axis=0, keepdims=True) * -keep)
        out_ref[r] = jnp.concatenate(rows, axis=0)

    each_row(x_ref.shape[0], one)


def inverse_kernel(vectors, outer, scale, facts, f_ref, wave_ref, out_ref):
    def one(r):
        length, inverse, norm = facts[0, r], facts[1, r], facts[2, r]
        wave = wave_ref[...]
        cos_in, sin_in, cos_out, sin_out = tables(wave, length, inverse, outer)
        weight = jnp.where(wave + wave < length, norm * scale, 0.0)
        weight = weight * jnp.where(wave == 0.0, 1.0, 2.0)
        four = f_ref[r] * weight
        real, imaginary = [], []
        for v in range(vectors):
            a, b = four[2 * v : 2 * v + 1], four[2 * v + 1 : 2 * v + 2]
            real.append(a * cos_out - b * sin_out)
            imaginary.append(-(a * sin_out + b * cos_out))
        values = dot_split(*both_halves(jnp.concatenate(real, axis=0)), *halves(cos_in), NT)
        values += dot_split(*both_halves(jnp.concatenate(imaginary, axis=0)), *halves(sin_in), NT)
        out_ref[r] = values * live_mask(length, vectors, outer)

    each_row(f_ref.shape[0], one)


def legendre_kernel(
    waves, used, span, place, low, four_ref, leg_ref, modes_ref, back_ref, rates_ref, spec_ref, out_ref
):
    step = pl.program_id(0)
    rows = four_ref.shape[1]
    fields = rows // 4
    pair_total = low.shape[0]
    first_pair = place[1]

    @pl.when(step == 0)
    def _():
        out_ref[...] = jnp.zeros_like(out_ref)

    base = (place[0] + step) * WIDTH
    pair = base // (waves + 1)
    column = base + lax.broadcasted_iota(jnp.int32, (1, WIDTH), 1)
    second = column >= (pair + 1) * (waves + 1)
    own_pair = jnp.where(second, pair + 1, pair)
    last = pair_total - 1
    low_wave = jnp.where(
        second, low[jnp.minimum(pair + 1, last)], low[jnp.minimum(pair, last)]
    )
    inside = column - own_pair * (waves + 1)
    low_length = waves - low_wave
    upper = inside >= low_length
    kind = jnp.where(upper, 2 + ((inside - low_length) & 1), inside & 1)
    degree = jnp.where(upper, inside - 1, low_wave + inside).astype(jnp.float32)
    valid = (own_pair >= first_pair) & (own_pair < first_pair + span) & (column < used)
    kind = jnp.where(valid, jnp.where(second, kind + 4, kind), 8)
    masks = [(kind == s).astype(jnp.float32) for s in range(8)]

    here = jnp.clip(pair - first_pair, 0, span - 1)
    there = jnp.clip(pair + 1 - first_pair, 0, span - 1)
    leg = jnp.where(column < used, leg_ref[...], 0.0)
    leg_high, leg_low = halves(leg)
    four = jnp.concatenate([four_ref[here], four_ref[there]], axis=0)
    product = dot_split(*both_halves(four), leg_high, leg_low, NN)
    raw = masks[0] * product[:fields]
    for s in range(1, 8):
        raw += masks[s] * product[s * fields : (s + 1) * fields]

    def mix(matrix, values):
        return lax.dot_general(
            matrix, values, NN, precision=HIGHEST, preferred_element_type=jnp.float32
        )

    eigen = degree * (degree + 1.0) * (1.0 / (waves * waves))
    projected = mix(modes_ref[...], raw) / (1.0 + rates_ref[...] * eigen)
    spectral = mix(back_ref[...], projected)
    spec_ref[...] = spectral
    parts = jnp.concatenate([masks[s] * spectral for s in range(8)], axis=0)
    sums = dot_split(*both_halves(parts), leg_high, leg_low, NT)
    out_ref[here] += sums[:rows]
    out_ref[there] += sums[rows:]


def smem():
    return pl.BlockSpec(memory_space=pltpu.SMEM)


def vmem():
    return pl.BlockSpec(memory_space=pltpu.VMEM)


def exchange(blocks, axes):
    shape = blocks.shape
    count = math.prod(shape[1:])
    dense = (shape[0], count // 128, 128) if count % 128 == 0 else (shape[0], 1, count)
    sent = lax.all_to_all(blocks.reshape(dense), axes, split_axis=0, concat_axis=0, tiled=True)
    return sent.reshape(shape)


def body(
    n_wave, n_lev, grid, row_points, lat_of_slot, pair_low, legendre, lat_weight, vert_modes, vert_back, vert_rates
):
    levels = grid.shape[0]
    ld = levels // n_lev
    waves = lat_of_slot.shape[0]
    half = waves // 2
    points = grid.shape[2] * n_wave
    lats = half // n_wave
    pair_count = legendre.shape[1] // (waves + 1)
    used = pair_count * (waves + 1)
    modes_pad = (used + 127) // 128 * 128
    span = -(-pair_count // n_lev)
    outer = -(-points // (INNER * 8)) * 8
    vectors = 2 * ld
    fields = 2 * levels
    devices = n_wave * n_lev
    wave_index = lax.axis_index("wave")
    lev_index = lax.axis_index("lev")

    low_blocks = pair_low.reshape(n_wave, pair_count)
    order = jnp.stack([low_blocks, waves - 1 - low_blocks], axis=2)
    order = jnp.pad(
        order, ((0, 0), (0, n_lev * span - pair_count), (0, 0)), constant_values=points
    )
    order = order.reshape(1, devices * span * 2).astype(jnp.float32)
    columns = order.shape[1]
    my_points = lax.dynamic_slice_in_dim(row_points, wave_index * lats, lats).astype(jnp.float32)
    facts = jnp.stack([my_points, 1.0 / my_points, lax.rsqrt(my_points)])
    parts = 2 if lats % 2 == 0 else 1
    some = lats // parts
    facts = [facts[:, k * some : (k + 1) * some] for k in range(parts)]

    lat_idx = jnp.arange(half, dtype=jnp.int32).reshape(n_wave, parts, some).transpose(1, 0, 2)
    lat_idx = lat_idx.reshape(half, 1)
    north = (lat_of_slot[None, :] == lat_idx).astype(jnp.float32)
    south = (lat_of_slot[None, :] == waves - 1 - lat_idx).astype(jnp.float32)
    unfold = jnp.stack([north + south, north - south], axis=1)
    weight = lat_weight.reshape(n_wave, parts, some).transpose(1, 0, 2).reshape(half, 1, 1)
    fold = (unfold * weight).reshape(parts, waves // parts, waves)
    unfold = unfold.reshape(waves, waves)

    params = pltpu.CompilerParams(vmem_limit_bytes=48 * 1024 * 1024)
    cost = pl.CostEstimate(flops=some * 2 * 10**8, bytes_accessed=2 * 10**6, transcendentals=0)
    whole = lax.all_to_all(grid, "lev", split_axis=0, concat_axis=1, tiled=True)
    pieces = []
    for k in range(parts):
        folded = jnp.einsum("xs,lsj->lxj", fold[k], whole, precision=HIGHEST)
        pieces.append(lax.all_to_all(folded, "wave", split_axis=1, concat_axis=2, tiled=True))
    arrived = []
    for k in range(parts):
        rows_in = pieces[k].reshape(ld, some, 2, points).transpose(1, 2, 0, 3)
        rows_in = jnp.pad(rows_in, ((0, 0), (0, 0), (0, 0), (0, outer * INNER - points)))
        rows_in = rows_in.reshape(some, vectors * outer, INNER)
        fourier = pl.pallas_call(
            functools.partial(forward_kernel, vectors, outer),
            out_shape=jax.ShapeDtypeStruct((some, 2 * vectors, columns), jnp.float32),
            in_specs=[smem(), vmem(), vmem()],
            out_specs=vmem(),
            compiler_params=params,
            cost_estimate=cost,
            name="forward_rows",
        )(facts[k], rows_in, order)
        fourier = fourier.reshape(some, 2, ld, 2, devices, 2 * span).transpose(4, 5, 1, 2, 3, 0)
        arrived.append(
            exchange(fourier, BOTH).reshape(n_wave, n_lev, span, 2, 2, ld, 2, some)
        )
    four = jnp.stack(arrived, axis=7).transpose(2, 3, 4, 1, 5, 6, 0, 7, 8)
    four = four.reshape(span, 4 * fields, half)

    starts = [min(l * span * (waves + 1), used - 1) // WIDTH for l in range(n_lev)]
    stops = [-(-min((l + 1) * span * (waves + 1), used) // WIDTH) for l in range(n_lev)]
    steps = max(1, max(b - a for a, b in zip(starts, stops)))
    final_block = (used - 1) // WIDTH
    start = jnp.minimum(lev_index * span * (waves + 1), used - 1) // WIDTH
    place = jnp.stack([start, lev_index * span]).astype(jnp.int32)
    my_low = lax.dynamic_slice_in_dim(pair_low, wave_index * pair_count, pair_count)
    pair_eye = jnp.eye(2, dtype=jnp.float32)
    grow = lambda m: (m[:, None, :, None] * pair_eye[None, :, None, :]).reshape(fields, fields)
    rates = jnp.repeat(vert_rates, 2)[:, None]
    fixed = lambda *shape: pl.BlockSpec(shape, lambda t, *_: (0,) * len(shape))
    spec, back = pl.pallas_call(
        functools.partial(legendre_kernel, waves, used, span),
        out_shape=(
            jax.ShapeDtypeStruct((fields, steps * WIDTH), jnp.float32),
            jax.ShapeDtypeStruct((span, 4 * fields, half), jnp.float32),
        ),
        grid_spec=pltpu.PrefetchScalarGridSpec(
            num_scalar_prefetch=2,
            grid=(steps,),
            in_specs=[
                fixed(span, 4 * fields, half),
                pl.BlockSpec(
                    (half, WIDTH), lambda t, p, _: (0, jnp.minimum(p[0] + t, final_block))
                ),
                fixed(fields, fields),
                fixed(fields, fields),
                fixed(fields, 1),
            ],
            out_specs=[
                pl.BlockSpec((fields, WIDTH), lambda t, *_: (0, t)),
                fixed(span, 4 * fields, half),
            ],
        ),
        compiler_params=params,
        name="legendre_both",
    )(place, my_low, four, legendre, grow(vert_modes), grow(vert_back), rates)

    back = back.reshape(span, 2, 2, n_lev, ld, 2, n_wave, parts, some)
    back = back.transpose(7, 6, 3, 0, 1, 2, 4, 5, 8)
    back = back.reshape(parts, devices, 2 * span, 2, ld, 2, some)
    returned = [exchange(back[k], BOTH) for k in range(parts)]

    pieces = lax.all_to_all(
        spec.reshape(n_lev, fields // n_lev, steps * WIDTH), "lev", split_axis=0, concat_axis=0, tiled=True
    )
    full = (final_block + 1 + steps) * WIDTH
    spectral = sum(
        jnp.pad(pieces[l], ((0, 0), (starts[l] * WIDTH, full - (starts[l] + steps) * WIDTH)))
        for l in range(n_lev)
    )
    spectral = spectral[:, :modes_pad].reshape(ld, 2, modes_pad)

    finished = []
    for k in range(parts):
        columns_back = returned[k].transpose(5, 2, 3, 4, 0, 1).reshape(some, 2 * vectors, columns)
        values = pl.pallas_call(
            functools.partial(inverse_kernel, vectors, outer, 1.0 / math.sqrt(waves)),
            out_shape=jax.ShapeDtypeStruct((some, vectors * outer, INNER), jnp.float32),
            in_specs=[smem(), vmem(), vmem()],
            out_specs=vmem(),
            compiler_params=params,
            cost_estimate=cost,
            name="inverse_rows",
        )(facts[k], columns_back, order)
        values = values.reshape(some, 2, ld, outer * INNER)[..., :points]
        values = values.transpose(2, 0, 1, 3).reshape(ld, 2 * some, points)
        finished.append(lax.all_to_all(values, "wave", split_axis=2, concat_axis=1, tiled=True))
    values = jnp.concatenate(finished, axis=1)
    slots = jnp.einsum("xs,lxj->lsj", unfold, values, precision=HIGHEST)
    grid_out = lax.all_to_all(slots, "lev", split_axis=1, concat_axis=0, tiled=True)
    return spectral, grid_out


def solution(mesh):
    placed = (P(None, "lev", "wave"), P(), P(), P(), P(None, "wave"), P(), P(), P(), P())
    return jax.shard_map(
        functools.partial(body, mesh.shape["wave"], mesh.shape["lev"]),
        mesh=mesh,
        in_specs=placed,
        out_specs=(P("lev", None, "wave"), P(None, "lev", "wave")),
        check_vma=False,
    )
```

```python
import functools
import math

import jax
import jax.numpy as jnp
import numpy as np
from jax import lax
from jax.experimental import pallas as pl
from jax.experimental.pallas import tpu as pltpu
from jax.sharding import PartitionSpec as P

HIGHEST = lax.Precision.HIGHEST
BOTH = ("wave", "lev")
INNER = 64
WIDTH = 640
NN = (((1,), (0,)), ((), ()))
NT = (((1,), (1,)), ((), ()))


def half_turn_fit():
    nodes = 0.5 * np.cos(np.pi * (np.arange(400) + 0.5) / 800)
    square = nodes**2
    sine = np.linalg.lstsq(
        np.vander(square, 5, increasing=True), np.sin(np.pi * nodes) / nodes, rcond=None
    )[0]
    cosine = np.linalg.lstsq(
        np.vander(square, 6, increasing=True), np.cos(np.pi * nodes), rcond=None
    )[0]
    return [round(float(c), 10) for c in sine], [round(float(c), 10) for c in cosine]


SINE, COSINE = half_turn_fit()


def poly(coefs, square):
    total = coefs[-1] * square + coefs[-2]
    for c in coefs[-3::-1]:
        total = total * square + c
    return total


def turn(product, length, inverse):
    rest = product - jnp.floor(product * inverse + 0.5) * length
    part = rest * inverse
    square = part * part
    sine = poly(SINE, square) * part
    cosine = poly(COSINE, square)
    double = sine + sine
    return 1.0 - double * sine, double * cosine


def halves(x):
    high = x.astype(jnp.bfloat16)
    return high, (x - high.astype(jnp.float32)).astype(jnp.bfloat16)


def both_halves(x):
    high = x.astype(jnp.bfloat16).astype(jnp.float32)
    return jnp.concatenate([high, x - high], axis=0).astype(jnp.bfloat16), high.astype(jnp.bfloat16)


def dot(a, b, dims):
    return lax.dot_general(a, b, dims, preferred_element_type=jnp.float32)


def dot_split(stacked, high, b_high, b_low, dims):
    rows = high.shape[0]
    first = dot(stacked, b_high, dims)
    return first[:rows] + first[rows:] + dot(high, b_low, dims)


def row_iota(rows):
    return lax.broadcasted_iota(jnp.int32, (rows, 1), 0)


def live_mask(length, vectors, outer):
    row = row_iota(vectors * outer) % outer
    position = row * INNER + lax.broadcasted_iota(jnp.int32, (vectors * outer, INNER), 1)
    return (position.astype(jnp.float32) < length).astype(jnp.float32)


def angle_sums(cos_base, sin_base, cos_step, sin_step):
    cos_rows, sin_rows = [], []
    for k in range(cos_step.shape[0]):
        c, s = cos_step[k : k + 1], sin_step[k : k + 1]
        cos_rows.append(cos_base * c - sin_base * s)
        sin_rows.append(sin_base * c + cos_base * s)
    return jnp.concatenate(cos_rows, axis=0), jnp.concatenate(sin_rows, axis=0)


def tables(wave, length, inverse, outer):
    row = row_iota(32)
    scale = jnp.where(row < 16, jnp.where(row < 8, 1, 8), jnp.where(row < 24, 64, 512))
    multiple = ((row & 7) * scale).astype(jnp.float32)
    c, s = turn(multiple * wave, length, inverse)
    top = 24 + outer // 8
    return angle_sums(c[:8], s[:8], c[8:16], s[8:16]) + angle_sums(
        c[16:24], s[16:24], c[24:top], s[24:top]
    )


def each_row(rows, one):
    together = 2 if rows % 2 == 0 else 1

    def some(step, carry):
        for k in range(together):
            one(step * together + k)
        return carry

    lax.fori_loop(0, rows // together, some, 0)


def forward_kernel(vectors, outer, facts, x_ref, wave_ref, out_ref):
    def one(r):
        length, inverse, norm = facts[0, r], facts[1, r], facts[2, r]
        wave = wave_ref[...]
        cos_in, sin_in, cos_out, sin_out = tables(wave, length, inverse, outer)
        x = x_ref[r] * live_mask(length, vectors, outer)
        stacked, high = both_halves(x)
        along = dot_split(stacked, high, *halves(cos_in), NN)
        across = dot_split(stacked, high, *halves(sin_in), NN)
        keep = jnp.where(wave + wave < length, norm, 0.0)
        rows = []
        for v in range(vectors):
            p, q = along[v * outer : (v + 1) * outer], across[v * outer : (v + 1) * outer]
            rows.append(jnp.sum(p * cos_out - q * sin_out, axis=0, keepdims=True) * keep)
            rows.append(jnp.sum(q * cos_out + p * sin_out, axis=0, keepdims=True) * -keep)
        out_ref[r] = jnp.concatenate(rows, axis=0)

    each_row(x_ref.shape[0], one)


def inverse_kernel(vectors, outer, scale, facts, f_ref, wave_ref, out_ref):
    def one(r):
        length, inverse, norm = facts[0, r], facts[1, r], facts[2, r]
        wave = wave_ref[...]
        cos_in, sin_in, cos_out, sin_out = tables(wave, length, inverse, outer)
        weight = jnp.where(wave + wave < length, norm * scale, 0.0)
        weight = weight * jnp.where(wave == 0.0, 1.0, 2.0)
        four = f_ref[r] * weight
        real, imaginary = [], []
        for v in range(vectors):
            a, b = four[2 * v : 2 * v + 1], four[2 * v + 1 : 2 * v + 2]
            real.append(a * cos_out - b * sin_out)
            imaginary.append(-(a * sin_out + b * cos_out))
        values = dot_split(*both_halves(jnp.concatenate(real, axis=0)), *halves(cos_in), NT)
        values += dot_split(*both_halves(jnp.concatenate(imaginary, axis=0)), *halves(sin_in), NT)
        out_ref[r] = values * live_mask(length, vectors, outer)

    each_row(f_ref.shape[0], one)


def legendre_kernel(
    waves, used, span, place, low, sym_ref, anti_ref, leg_ref, modes_ref, back_ref, rates_ref, spec_ref, even_ref, odd_ref
):
    step = pl.program_id(0)
    rows = sym_ref.shape[1]
    fields = rows // 2
    pair_total = low.shape[0]
    first_pair = place[1]

    @pl.when(step == 0)
    def _():
        even_ref[...] = jnp.zeros_like(even_ref)
        odd_ref[...] = jnp.zeros_like(odd_ref)

    base = (place[0] + step) * WIDTH
    pair = base // (waves + 1)
    column = base + lax.broadcasted_iota(jnp.int32, (1, WIDTH), 1)
    second = column >= (pair + 1) * (waves + 1)
    own_pair = jnp.where(second, pair + 1, pair)
    last = pair_total - 1
    low_wave = jnp.where(
        second, low[jnp.minimum(pair + 1, last)], low[jnp.minimum(pair, last)]
    )
    inside = column - own_pair * (waves + 1)
    low_length = waves - low_wave
    upper = inside >= low_length
    kind = jnp.where(upper, 1 + 2 * ((inside - low_length) & 1), 2 * (inside & 1))
    degree = jnp.where(upper, inside - 1, low_wave + inside).astype(jnp.float32)
    valid = (own_pair >= first_pair) & (own_pair < first_pair + span) & (column < used)
    kind = jnp.where(valid, jnp.where(second, kind + 4, kind), 8)
    masks = [(kind == s).astype(jnp.float32) for s in range(8)]

    here = jnp.clip(pair - first_pair, 0, span - 1)
    there = jnp.clip(pair + 1 - first_pair, 0, span - 1)
    leg = jnp.where(column < used, leg_ref[...], 0.0)
    leg_high, leg_low = halves(leg)
    four = jnp.concatenate(
        [sym_ref[here], anti_ref[here], sym_ref[there], anti_ref[there]], axis=0
    )
    product = dot_split(*both_halves(four), leg_high, leg_low, NN)
    raw = masks[0] * product[:fields]
    for s in range(1, 8):
        raw += masks[s] * product[s * fields : (s + 1) * fields]

    def mix(matrix, values):
        return lax.dot_general(
            matrix, values, NN, precision=HIGHEST, preferred_element_type=jnp.float32
        )

    eigen = degree * (degree + 1.0) * (1.0 / (waves * waves))
    projected = mix(modes_ref[...], raw) / (1.0 + rates_ref[...] * eigen)
    spectral = mix(back_ref[...], projected)
    spec_ref[...] = spectral
    parts = jnp.concatenate([masks[s] * spectral for s in range(8)], axis=0)
    sums = dot_split(*both_halves(parts), leg_high, leg_low, NT)
    even_ref[here] += sums[:rows]
    odd_ref[here] += sums[rows : 2 * rows]
    even_ref[there] += sums[2 * rows : 3 * rows]
    odd_ref[there] += sums[3 * rows :]


def smem():
    return pl.BlockSpec(memory_space=pltpu.SMEM)


def vmem():
    return pl.BlockSpec(memory_space=pltpu.VMEM)


def exchange(blocks, axes):
    shape = blocks.shape
    count = math.prod(shape[1:])
    dense = (shape[0], count // 128, 128) if count % 128 == 0 else (shape[0], 1, count)
    sent = lax.all_to_all(blocks.reshape(dense), axes, split_axis=0, concat_axis=0, tiled=True)
    return sent.reshape(shape)


def body(
    n_wave, n_lev, grid, row_points, lat_of_slot, pair_low, legendre, lat_weight, vert_modes, vert_back, vert_rates
):
    levels, slots_lev, chunk = grid.shape
    ld = levels // n_lev
    waves = lat_of_slot.shape[0]
    half = waves // 2
    points = chunk * n_wave
    pair_count = legendre.shape[1] // (waves + 1)
    used = pair_count * (waves + 1)
    modes_pad = (used + 127) // 128 * 128
    span = -(-pair_count // n_lev)
    outer = -(-points // (INNER * 8)) * 8
    fields = 2 * levels
    devices = n_wave * n_lev
    some = -(-slots_lev // n_wave)
    spare = n_wave * some - slots_lev
    wave_index = lax.axis_index("wave")
    lev_index = lax.axis_index("lev")

    low_blocks = pair_low.reshape(n_wave, pair_count)
    order = jnp.stack([low_blocks, waves - 1 - low_blocks], axis=2)
    order = jnp.pad(
        order, ((0, 0), (0, n_lev * span - pair_count), (0, 0)), constant_values=points
    )
    order = order.reshape(1, devices * span * 2).astype(jnp.float32)
    columns = order.shape[1]
    blocks = jnp.pad(grid, ((0, 0), (0, spare), (0, 0))).reshape(levels, n_wave, some, chunk)
    blocks = blocks.transpose(1, 0, 2, 3).reshape(n_wave, levels * some, chunk)
    rows_in = lax.all_to_all(blocks, "wave", split_axis=0, concat_axis=0, tiled=True)

    held = jnp.minimum(wave_index * some + jnp.arange(some), slots_lev - 1)
    my_points = row_points[lat_of_slot[lev_index * slots_lev + held]].astype(jnp.float32)
    facts = jnp.stack([my_points, 1.0 / my_points, lax.rsqrt(my_points)])

    lat_held = jnp.pad(
        lat_of_slot.reshape(n_lev, slots_lev), ((0, 0), (0, spare)), constant_values=-1
    ).reshape(1, -1)
    slots = lat_held.shape[1]
    lat_idx = jnp.arange(half, dtype=jnp.int32)[:, None]
    north = (lat_held == lat_idx).astype(jnp.float32)
    south = (lat_held == waves - 1 - lat_idx).astype(jnp.float32)
    both, apart = north + south, north - south

    params = pltpu.CompilerParams(vmem_limit_bytes=48 * 1024 * 1024)
    rows_in = rows_in.reshape(n_wave, levels, some, chunk).transpose(2, 1, 0, 3)
    rows_in = rows_in.reshape(some, levels, points)
    rows_in = jnp.pad(rows_in, ((0, 0), (0, 0), (0, outer * INNER - points)))
    rows_in = rows_in.reshape(some, levels * outer, INNER)
    fourier = pl.pallas_call(
        functools.partial(forward_kernel, levels, outer),
        out_shape=jax.ShapeDtypeStruct((some, fields, columns), jnp.float32),
        in_specs=[smem(), vmem(), vmem()],
        out_specs=vmem(),
        compiler_params=params,
        name="forward_rows",
    )(facts, rows_in, order)
    fourier = fourier.reshape(some, fields, devices, 2 * span).transpose(2, 3, 1, 0)
    arrived = exchange(fourier, BOTH).reshape(n_wave, n_lev, 2 * span * fields, some)
    arrived = arrived.transpose(2, 1, 0, 3).reshape(2 * span * fields, slots)
    symmetric = jnp.einsum("cs,rs->cr", arrived, both, precision=HIGHEST) * lat_weight
    antisymmetric = jnp.einsum("cs,rs->cr", arrived, apart, precision=HIGHEST) * lat_weight
    symmetric = symmetric.reshape(span, 2 * fields, half)
    antisymmetric = antisymmetric.reshape(span, 2 * fields, half)

    starts = [min(l * span * (waves + 1), used - 1) // WIDTH for l in range(n_lev)]
    stops = [-(-min((l + 1) * span * (waves + 1), used) // WIDTH) for l in range(n_lev)]
    steps = max(1, max(b - a for a, b in zip(starts, stops)))
    final_block = (used - 1) // WIDTH
    start = jnp.minimum(lev_index * span * (waves + 1), used - 1) // WIDTH
    place = jnp.stack([start, lev_index * span]).astype(jnp.int32)
    my_low = lax.dynamic_slice_in_dim(pair_low, wave_index * pair_count, pair_count)
    pair_eye = jnp.eye(2, dtype=jnp.float32)
    grow = lambda m: (m[:, None, :, None] * pair_eye[None, :, None, :]).reshape(fields, fields)
    rates = jnp.repeat(vert_rates, 2)[:, None]
    fixed = lambda *shape: pl.BlockSpec(shape, lambda t, *_: (0,) * len(shape))
    spec, even, odd = pl.pallas_call(
        functools.partial(legendre_kernel, waves, used, span),
        out_shape=(
            jax.ShapeDtypeStruct((fields, steps * WIDTH), jnp.float32),
            jax.ShapeDtypeStruct((span, 2 * fields, half), jnp.float32),
            jax.ShapeDtypeStruct((span, 2 * fields, half), jnp.float32),
        ),
        grid_spec=pltpu.PrefetchScalarGridSpec(
            num_scalar_prefetch=2,
            grid=(steps,),
            in_specs=[
                fixed(span, 2 * fields, half),
                fixed(span, 2 * fields, half),
                pl.BlockSpec(
                    (half, WIDTH), lambda t, p, _: (0, jnp.minimum(p[0] + t, final_block))
                ),
                fixed(fields, fields),
                fixed(fields, fields),
                fixed(fields, 1),
            ],
            out_specs=[
                pl.BlockSpec((fields, WIDTH), lambda t, *_: (0, t)),
                fixed(span, 2 * fields, half),
                fixed(span, 2 * fields, half),
            ],
        ),
        compiler_params=params,
        name="legendre_both",
    )(place, my_low, symmetric, antisymmetric, legendre, grow(vert_modes), grow(vert_back), rates)

    by_slot = jnp.einsum("cfr,rs->cfs", even, both, precision=HIGHEST)
    by_slot += jnp.einsum("cfr,rs->cfs", odd, apart, precision=HIGHEST)
    by_slot = by_slot.reshape(2 * span * fields, n_lev, n_wave, some).transpose(2, 1, 0, 3)
    returned = exchange(by_slot.reshape(devices, 2 * span, fields, some), BOTH)

    pieces = lax.all_to_all(
        spec.reshape(n_lev, fields // n_lev, steps * WIDTH), "lev", split_axis=0, concat_axis=0, tiled=True
    )
    full = (final_block + 1 + steps) * WIDTH
    spectral = sum(
        jnp.pad(pieces[l], ((0, 0), (starts[l] * WIDTH, full - (starts[l] + steps) * WIDTH)))
        for l in range(n_lev)
    )
    spectral = spectral[:, :modes_pad].reshape(ld, 2, modes_pad)

    returned = returned.transpose(3, 2, 0, 1).reshape(some, fields, columns)
    values = pl.pallas_call(
        functools.partial(inverse_kernel, levels, outer, 1.0 / math.sqrt(waves)),
        out_shape=jax.ShapeDtypeStruct((some, levels * outer, INNER), jnp.float32),
        in_specs=[smem(), vmem(), vmem()],
        out_specs=vmem(),
        compiler_params=params,
        name="inverse_rows",
    )(facts, returned, order)
    values = values.reshape(some, levels, outer * INNER)[..., :points]
    values = values.reshape(some, levels, n_wave, chunk).transpose(2, 1, 0, 3)
    values = values.reshape(n_wave, levels * some, chunk)
    values = lax.all_to_all(values, "wave", split_axis=0, concat_axis=0, tiled=True)
    values = values.reshape(n_wave, levels, some, chunk).transpose(1, 0, 2, 3)
    grid_out = values.reshape(levels, n_wave * some, chunk)[:, :slots_lev]
    return spectral, grid_out


def solution(mesh):
    placed = (P(None, "lev", "wave"), P(), P(), P(), P(None, "wave"), P(), P(), P(), P())
    return jax.shard_map(
        functools.partial(body, mesh.shape["wave"], mesh.shape["lev"]),
        mesh=mesh,
        in_specs=placed,
        out_specs=(P("lev", None, "wave"), P(None, "lev", "wave")),
        check_vma=False,
    )
```

```python
import functools
import math

import jax
import jax.numpy as jnp
import numpy as np
from jax import lax
from jax.experimental import pallas as pl
from jax.experimental.pallas import tpu as pltpu
from jax.sharding import PartitionSpec as P

HIGHEST = lax.Precision.HIGHEST
BOTH = ("wave", "lev")
INNER = 64
WIDTH = 640
NN = (((1,), (0,)), ((), ()))
NT = (((1,), (1,)), ((), ()))


def half_turn_fit():
    nodes = 0.5 * np.cos(np.pi * (np.arange(400) + 0.5) / 800)
    square = nodes**2
    sine = np.linalg.lstsq(
        np.vander(square, 5, increasing=True), np.sin(np.pi * nodes) / nodes, rcond=None
    )[0]
    cosine = np.linalg.lstsq(
        np.vander(square, 6, increasing=True), np.cos(np.pi * nodes), rcond=None
    )[0]
    return [round(float(c), 10) for c in sine], [round(float(c), 10) for c in cosine]


SINE, COSINE = half_turn_fit()


def poly(coefs, square):
    total = coefs[-1] * square + coefs[-2]
    for c in coefs[-3::-1]:
        total = total * square + c
    return total


def turn(product, length, inverse):
    rest = product - jnp.floor(product * inverse + 0.5) * length
    part = rest * inverse
    square = part * part
    sine = poly(SINE, square) * part
    cosine = poly(COSINE, square)
    double = sine + sine
    return 1.0 - double * sine, double * cosine


def halves(x):
    high = x.astype(jnp.bfloat16)
    return high, (x - high.astype(jnp.float32)).astype(jnp.bfloat16)


def both_halves(x):
    high = x.astype(jnp.bfloat16).astype(jnp.float32)
    return jnp.concatenate([high, x - high], axis=0).astype(jnp.bfloat16), high.astype(jnp.bfloat16)


def dot(a, b, dims):
    return lax.dot_general(a, b, dims, preferred_element_type=jnp.float32)


def dot_split(stacked, high, b_high, b_low, dims):
    rows = high.shape[0]
    first = dot(stacked, b_high, dims)
    return first[:rows] + first[rows:] + dot(high, b_low, dims)


def row_iota(rows):
    return lax.broadcasted_iota(jnp.int32, (rows, 1), 0)


def live_mask(length, vectors, outer):
    row = row_iota(vectors * outer) % outer
    position = row * INNER + lax.broadcasted_iota(jnp.int32, (vectors * outer, INNER), 1)
    return (position.astype(jnp.float32) < length).astype(jnp.float32)


def angle_sums(cos_base, sin_base, cos_step, sin_step):
    cos_rows, sin_rows = [], []
    for k in range(cos_step.shape[0]):
        c, s = cos_step[k : k + 1], sin_step[k : k + 1]
        cos_rows.append(cos_base * c - sin_base * s)
        sin_rows.append(sin_base * c + cos_base * s)
    return jnp.concatenate(cos_rows, axis=0), jnp.concatenate(sin_rows, axis=0)


def tables(wave, length, inverse, outer):
    row = row_iota(32)
    scale = jnp.where(row < 16, jnp.where(row < 8, 1, 8), jnp.where(row < 24, 64, 512))
    multiple = ((row & 7) * scale).astype(jnp.float32)
    c, s = turn(multiple * wave, length, inverse)
    top = 24 + outer // 8
    return angle_sums(c[:8], s[:8], c[8:16], s[8:16]) + angle_sums(
        c[16:24], s[16:24], c[24:top], s[24:top]
    )


def each_row(rows, one):
    together = 2 if rows % 2 == 0 else 1

    def some(step, carry):
        for k in range(together):
            one(step * together + k)
        return carry

    lax.fori_loop(0, rows // together, some, 0)


def forward_kernel(vectors, outer, facts, x_ref, wave_ref, out_ref):
    def one(r):
        length, inverse, norm = facts[0, r], facts[1, r], facts[2, r]
        wave = wave_ref[...]
        cos_in, sin_in, cos_out, sin_out = tables(wave, length, inverse, outer)
        x = x_ref[r] * live_mask(length, vectors, outer)
        stacked, high = both_halves(x)
        along = dot_split(stacked, high, *halves(cos_in), NN)
        across = dot_split(stacked, high, *halves(sin_in), NN)
        keep = jnp.where(wave + wave < length, norm, 0.0)
        rows = []
        for v in range(vectors):
            p, q = along[v * outer : (v + 1) * outer], across[v * outer : (v + 1) * outer]
            rows.append(jnp.sum(p * cos_out - q * sin_out, axis=0, keepdims=True) * keep)
            rows.append(jnp.sum(q * cos_out + p * sin_out, axis=0, keepdims=True) * -keep)
        out_ref[r] = jnp.concatenate(rows, axis=0)

    each_row(x_ref.shape[0], one)


def inverse_kernel(vectors, outer, scale, facts, f_ref, wave_ref, out_ref):
    def one(r):
        length, inverse, norm = facts[0, r], facts[1, r], facts[2, r]
        wave = wave_ref[...]
        cos_in, sin_in, cos_out, sin_out = tables(wave, length, inverse, outer)
        weight = jnp.where(wave + wave < length, norm * scale, 0.0)
        weight = weight * jnp.where(wave == 0.0, 1.0, 2.0)
        four = f_ref[r] * weight
        real, imaginary = [], []
        for v in range(vectors):
            a, b = four[2 * v : 2 * v + 1], four[2 * v + 1 : 2 * v + 2]
            real.append(a * cos_out - b * sin_out)
            imaginary.append(-(a * sin_out + b * cos_out))
        values = dot_split(*both_halves(jnp.concatenate(real, axis=0)), *halves(cos_in), NT)
        values += dot_split(*both_halves(jnp.concatenate(imaginary, axis=0)), *halves(sin_in), NT)
        out_ref[r] = values * live_mask(length, vectors, outer)

    each_row(f_ref.shape[0], one)


def legendre_kernel(
    waves, used, span, place, low, sym_ref, anti_ref, leg_ref, modes_ref, back_ref, rates_ref, spec_ref, even_ref, odd_ref
):
    step = pl.program_id(0)
    rows = sym_ref.shape[1]
    fields = rows // 2
    pair_total = low.shape[0]
    first_pair = place[1]

    @pl.when(step == 0)
    def _():
        even_ref[...] = jnp.zeros_like(even_ref)
        odd_ref[...] = jnp.zeros_like(odd_ref)

    base = (place[0] + step) * WIDTH
    pair = base // (waves + 1)
    column = base + lax.broadcasted_iota(jnp.int32, (1, WIDTH), 1)
    second = column >= (pair + 1) * (waves + 1)
    own_pair = jnp.where(second, pair + 1, pair)
    last = pair_total - 1
    low_wave = jnp.where(
        second, low[jnp.minimum(pair + 1, last)], low[jnp.minimum(pair, last)]
    )
    inside = column - own_pair * (waves + 1)
    low_length = waves - low_wave
    upper = inside >= low_length
    kind = jnp.where(upper, 1 + 2 * ((inside - low_length) & 1), 2 * (inside & 1))
    degree = jnp.where(upper, inside - 1, low_wave + inside).astype(jnp.float32)
    valid = (own_pair >= first_pair) & (own_pair < first_pair + span) & (column < used)
    kind = jnp.where(valid, jnp.where(second, kind + 4, kind), 8)
    masks = [(kind == s).astype(jnp.float32) for s in range(8)]

    here = jnp.clip(pair - first_pair, 0, span - 1)
    there = jnp.clip(pair + 1 - first_pair, 0, span - 1)
    leg = jnp.where(column < used, leg_ref[...], 0.0)
    leg_high, leg_low = halves(leg)
    four = jnp.concatenate(
        [sym_ref[here], anti_ref[here], sym_ref[there], anti_ref[there]], axis=0
    )
    product = dot_split(*both_halves(four), leg_high, leg_low, NN)
    raw = masks[0] * product[:fields]
    for s in range(1, 8):
        raw += masks[s] * product[s * fields : (s + 1) * fields]

    def mix(matrix, values):
        return lax.dot_general(
            matrix, values, NN, precision=HIGHEST, preferred_element_type=jnp.float32
        )

    eigen = degree * (degree + 1.0) * (1.0 / (waves * waves))
    projected = mix(modes_ref[...], raw) / (1.0 + rates_ref[...] * eigen)
    spectral = mix(back_ref[...], projected)
    spec_ref[...] = spectral
    parts = jnp.concatenate([masks[s] * spectral for s in range(8)], axis=0)
    sums = dot_split(*both_halves(parts), leg_high, leg_low, NT)
    even_ref[here] += sums[:rows]
    odd_ref[here] += sums[rows : 2 * rows]
    even_ref[there] += sums[2 * rows : 3 * rows]
    odd_ref[there] += sums[3 * rows :]


def smem():
    return pl.BlockSpec(memory_space=pltpu.SMEM)


def vmem():
    return pl.BlockSpec(memory_space=pltpu.VMEM)


def exchange(blocks, axes):
    shape = blocks.shape
    count = math.prod(shape[1:])
    dense = (shape[0], count // 128, 128) if count % 128 == 0 else (shape[0], 1, count)
    sent = lax.all_to_all(blocks.reshape(dense), axes, split_axis=0, concat_axis=0, tiled=True)
    return sent.reshape(shape)


def body(
    n_wave, n_lev, grid, row_points, lat_of_slot, pair_low, legendre, lat_weight, vert_modes, vert_back, vert_rates
):
    levels, slots_lev, chunk = grid.shape
    ld = levels // n_lev
    waves = lat_of_slot.shape[0]
    half = waves // 2
    points = chunk * n_wave
    pair_count = legendre.shape[1] // (waves + 1)
    used = pair_count * (waves + 1)
    modes_pad = (used + 127) // 128 * 128
    span = -(-pair_count // n_lev)
    outer = -(-points // (INNER * 8)) * 8
    fields = 2 * levels
    devices = n_wave * n_lev
    some = -(-slots_lev // n_wave)
    spare = n_wave * some - slots_lev
    wave_index = lax.axis_index("wave")
    lev_index = lax.axis_index("lev")

    low_blocks = pair_low.reshape(n_wave, pair_count)
    order = jnp.stack([low_blocks, waves - 1 - low_blocks], axis=2)
    order = jnp.pad(
        order, ((0, 0), (0, n_lev * span - pair_count), (0, 0)), constant_values=points
    )
    order = order.reshape(1, devices * span * 2).astype(jnp.float32)
    columns = order.shape[1]
    blocks = jnp.pad(grid, ((0, 0), (0, spare), (0, 0))).reshape(levels, n_wave, some, chunk)
    blocks = blocks.transpose(1, 0, 2, 3).reshape(n_wave, levels * some, chunk)
    rows_in = lax.all_to_all(blocks, "wave", split_axis=0, concat_axis=0, tiled=True)

    held = jnp.minimum(wave_index * some + jnp.arange(some), slots_lev - 1)
    my_points = row_points[lat_of_slot[lev_index * slots_lev + held]].astype(jnp.float32)
    facts = jnp.stack([my_points, 1.0 / my_points, lax.rsqrt(my_points)])

    lat_held = jnp.pad(
        lat_of_slot.reshape(n_lev, slots_lev), ((0, 0), (0, spare)), constant_values=-1
    )
    lat_held = lat_held.reshape(n_lev, n_wave, some).transpose(1, 0, 2).reshape(1, -1)
    slots = lat_held.shape[1]
    lat_idx = jnp.arange(half, dtype=jnp.int32)[:, None]
    north = (lat_held == lat_idx).astype(jnp.float32)
    south = (lat_held == waves - 1 - lat_idx).astype(jnp.float32)
    both, apart = north + south, north - south

    params = pltpu.CompilerParams(vmem_limit_bytes=48 * 1024 * 1024)
    rows_in = rows_in.reshape(n_wave, levels, some, chunk).transpose(2, 1, 0, 3)
    rows_in = rows_in.reshape(some, levels, points)
    rows_in = jnp.pad(rows_in, ((0, 0), (0, 0), (0, outer * INNER - points)))
    rows_in = rows_in.reshape(some, levels * outer, INNER)
    fourier = pl.pallas_call(
        functools.partial(forward_kernel, levels, outer),
        out_shape=jax.ShapeDtypeStruct((some, fields, columns), jnp.float32),
        in_specs=[smem(), vmem(), vmem()],
        out_specs=vmem(),
        compiler_params=params,
        name="forward_rows",
    )(facts, rows_in, order)
    fourier = lax.optimization_barrier(fourier.transpose(1, 0, 2).reshape(fields * some, columns))
    fourier = lax.optimization_barrier(fourier.T).reshape(devices, 2 * span, fields, some)
    arrived = exchange(fourier, BOTH).reshape(devices, 2 * span * fields, some)
    arrived = arrived.transpose(1, 0, 2).reshape(2 * span * fields, slots)
    symmetric = jnp.einsum("cs,rs->cr", arrived, both, precision=HIGHEST) * lat_weight
    antisymmetric = jnp.einsum("cs,rs->cr", arrived, apart, precision=HIGHEST) * lat_weight
    symmetric = symmetric.reshape(span, 2 * fields, half)
    antisymmetric = antisymmetric.reshape(span, 2 * fields, half)

    starts = [min(l * span * (waves + 1), used - 1) // WIDTH for l in range(n_lev)]
    stops = [-(-min((l + 1) * span * (waves + 1), used) // WIDTH) for l in range(n_lev)]
    steps = max(1, max(b - a for a, b in zip(starts, stops)))
    final_block = (used - 1) // WIDTH
    start = jnp.minimum(lev_index * span * (waves + 1), used - 1) // WIDTH
    place = jnp.stack([start, lev_index * span]).astype(jnp.int32)
    my_low = lax.dynamic_slice_in_dim(pair_low, wave_index * pair_count, pair_count)
    pair_eye = jnp.eye(2, dtype=jnp.float32)
    grow = lambda m: (m[:, None, :, None] * pair_eye[None, :, None, :]).reshape(fields, fields)
    rates = jnp.repeat(vert_rates, 2)[:, None]
    fixed = lambda *shape: pl.BlockSpec(shape, lambda t, *_: (0,) * len(shape))
    spec, even, odd = pl.pallas_call(
        functools.partial(legendre_kernel, waves, used, span),
        out_shape=(
            jax.ShapeDtypeStruct((fields, steps * WIDTH), jnp.float32),
            jax.ShapeDtypeStruct((span, 2 * fields, half), jnp.float32),
            jax.ShapeDtypeStruct((span, 2 * fields, half), jnp.float32),
        ),
        grid_spec=pltpu.PrefetchScalarGridSpec(
            num_scalar_prefetch=2,
            grid=(steps,),
            in_specs=[
                fixed(span, 2 * fields, half),
                fixed(span, 2 * fields, half),
                pl.BlockSpec(
                    (half, WIDTH), lambda t, p, _: (0, jnp.minimum(p[0] + t, final_block))
                ),
                fixed(fields, fields),
                fixed(fields, fields),
                fixed(fields, 1),
            ],
            out_specs=[
                pl.BlockSpec((fields, WIDTH), lambda t, *_: (0, t)),
                fixed(span, 2 * fields, half),
                fixed(span, 2 * fields, half),
            ],
        ),
        compiler_params=params,
        name="legendre_both",
    )(place, my_low, symmetric, antisymmetric, legendre, grow(vert_modes), grow(vert_back), rates)

    turned = [
        x.reshape(2 * span, fields, half).transpose(1, 0, 2).reshape(fields * 2 * span, half)
        for x in (even, odd)
    ]
    by_slot = jnp.einsum("rs,cr->sc", both, turned[0], precision=HIGHEST)
    by_slot += jnp.einsum("rs,cr->sc", apart, turned[1], precision=HIGHEST)
    returned = exchange(by_slot.reshape(devices, some, fields, 2 * span), BOTH)

    pieces = lax.all_to_all(
        spec.reshape(n_lev, fields // n_lev, steps * WIDTH), "lev", split_axis=0, concat_axis=0, tiled=True
    )
    full = (final_block + 1 + steps) * WIDTH
    spectral = sum(
        jnp.pad(pieces[l], ((0, 0), (starts[l] * WIDTH, full - (starts[l] + steps) * WIDTH)))
        for l in range(n_lev)
    )
    spectral = spectral[:, :modes_pad].reshape(ld, 2, modes_pad)

    returned = returned.transpose(1, 2, 0, 3).reshape(some, fields, columns)
    values = pl.pallas_call(
        functools.partial(inverse_kernel, levels, outer, 1.0 / math.sqrt(waves)),
        out_shape=jax.ShapeDtypeStruct((some, levels * outer, INNER), jnp.float32),
        in_specs=[smem(), vmem(), vmem()],
        out_specs=vmem(),
        compiler_params=params,
        name="inverse_rows",
    )(facts, returned, order)
    values = values.reshape(some, levels, outer * INNER)[..., :points]
    values = values.reshape(some, levels, n_wave, chunk).transpose(2, 1, 0, 3)
    values = values.reshape(n_wave, levels * some, chunk)
    values = lax.all_to_all(values, "wave", split_axis=0, concat_axis=0, tiled=True)
    values = values.reshape(n_wave, levels, some, chunk).transpose(1, 0, 2, 3)
    grid_out = values.reshape(levels, n_wave * some, chunk)[:, :slots_lev]
    return spectral, grid_out


def solution(mesh):
    placed = (P(None, "lev", "wave"), P(), P(), P(), P(None, "wave"), P(), P(), P(), P())
    return jax.shard_map(
        functools.partial(body, mesh.shape["wave"], mesh.shape["lev"]),
        mesh=mesh,
        in_specs=placed,
        out_specs=(P("lev", None, "wave"), P(None, "lev", "wave")),
        check_vma=False,
    )
```
